32 devices in a mesh: blk: 16 (over z, x, core), tp: 2 (over y).
Axes of the slice: x: 2, y: 2, z: 4, core: 2. Of those that a mesh axis runs over, the one named last changes fastest.
Arguments:
- tokens: bfloat16 [4096, 8192], P('blk', 'tp'), may hold values from -6 to 6
- weight: bfloat16 [8192, 2048], P('tp'), may hold values from -0.0625 to 0.0625
- bank_a: bfloat16 [16, 8192, 32], P('blk', 'tp'), may hold values from -0.0625 to 0.0625
- bank_b: bfloat16 [16, 32, 1024], P('blk'), may hold values from -1.5 to 1.5
- tile_map: int32 [32, 1], P('blk'), may hold values from 0 to 15
- grad_out: bfloat16 [4096, 2048], P(('blk', 'tp')), may hold values from -6 to 6
Outputs:
- key_value_output: bfloat16 [4096, 2048], P(('blk', 'tp'))
- token_gradient: bfloat16 [4096, 8192], P('blk', 'tp')
- grad_a: float32 [16, 8192, 32], P('blk', 'tp')
- grad_b: float32 [16, 32, 1024], P('blk', None, 'tp')
The draws below stay inside these ranges and needn't reach their ends.
Inputs may be any that keep to these rules, and one draw needn't show every extreme that they name: `tile_map`: every one of the 16 adapters is the adapter of at least one tile.
All inputs are finite; a program needn't handle non-finite values.
Results may differ from the reference program's by a relative error of at most 0.003.
Values may be sent and summed in bfloat16 or wider, within the bound.
No kernel may reach another device: no remote copies, remote signals or barrier semaphores. Data moves between devices by JAX's collectives and lax.ppermute only.
A program may use at most 128 MiB of HBM per device.

```python
import jax
import jax.numpy as jnp
from jax import lax

MODEL_WIDTH = 8192
KEY_VALUE_WIDTH = 1024
RANK = 16
TILE = 128
ADAPTERS = 16
TILES = 32
TOKENS = 4096


def steps_of(key, extent, pieces, smallest, top_value):
    loudness, own = 1.0, jax.random.fold_in(key, 6)
    for position, shards_of in pieces:
        steps = jnp.exp(jax.random.uniform(jax.random.fold_in(own, position), (shards_of,), jnp.float32, smallest / len(pieces), top_value / len(pieces)))
        loudness = loudness * jnp.repeat(steps, extent[position] // shards_of).reshape([-1 if axis == position else 1 for axis in range(len(extent))])
    return loudness


def distinct(own_key, rows, number_of, top, lift):
    ranking = jax.random.permutation(jax.random.fold_in(own_key, 1), number_of)
    pull = ranking
    for power in range(3):
        pull = pull * pull // number_of
    pull = pull * lift // number_of
    chance = jax.random.randint(jax.random.fold_in(own_key, 2), (rows, number_of), 0, 4096) + pull
    fixed_rows = jax.random.permutation(jax.random.fold_in(own_key, 3), rows)[jnp.arange(number_of) % rows]
    chance = jnp.where(jnp.arange(rows)[:, None] == fixed_rows[None, :], 1 << 14, chance)
    merit = chance * number_of + jnp.arange(number_of)
    return lax.top_k(merit.astype(jnp.int32), top)[1].astype(jnp.int32)


def normal_values(stream_key, shape, deviation, limit, split=(), kind=jnp.bfloat16):
    result = deviation * jax.random.normal(stream_key, shape, jnp.float32)
    if split:
        result = result * steps_of(stream_key, shape, split, -0.22, 0.18)
    return jnp.clip(result, -limit, limit).astype(kind)


def setup_inputs(seed: int = 0) -> dict:
    key_list = jax.random.split(jax.random.key(seed), 7)
    tokens = normal_values(key_list[0], (TOKENS, MODEL_WIDTH), 1.0, 6.0, ((0, 16), (1, 2)))
    weight = normal_values(key_list[1], (MODEL_WIDTH, 2 * KEY_VALUE_WIDTH), MODEL_WIDTH ** -0.5, 0.0625, ((0, 2),))
    bank_a = normal_values(key_list[2], (ADAPTERS, MODEL_WIDTH, 2 * RANK), MODEL_WIDTH ** -0.5, 0.0625, ((0, 16), (1, 2)))
    bank_b = normal_values(key_list[3], (ADAPTERS, 2 * RANK, KEY_VALUE_WIDTH), RANK ** -0.5, 1.5, ((0, 16),))
    tile_map = distinct(key_list[4], TILES, ADAPTERS, 1, 1024)
    grad_out = normal_values(key_list[5], (TOKENS, 2 * KEY_VALUE_WIDTH), 1.0, 6.0, ((0, 32),))
    return {"tokens": tokens, "weight": weight, "bank_a": bank_a, "bank_b": bank_b, "tile_map": tile_map, "grad_out": grad_out}


adapter_scale = 0.5


def reference(tokens, weight, bank_a, bank_b, tile_map, grad_out):
    tile_index_list = tile_map[:, 0].astype(jnp.int32)
    overall_row_count = tokens.shape[0]
    tiles = overall_row_count // TILE
    token_tile_index = tokens.reshape(tiles, TILE, MODEL_WIDTH)
    gradient_per_tile = grad_out.reshape(tiles, TILE, 2 * KEY_VALUE_WIDTH)

    def single_tile(packed):
        token_rows, grad_rows, adapter = packed
        factor_down = bank_a[adapter]
        fac_b = bank_b[adapter]
        rank_act = jnp.dot(token_rows, factor_down, preferred_element_type=jnp.float32).astype(jnp.bfloat16)
        adapter_partial = jnp.concatenate([
            jnp.dot(rank_act[:, :RANK], fac_b[:RANK], preferred_element_type=jnp.float32),
            jnp.dot(rank_act[:, RANK:], fac_b[RANK:], preferred_element_type=jnp.float32)], axis=1)
        low_rank_gradient = jnp.concatenate([
            jnp.dot(grad_rows[:, :KEY_VALUE_WIDTH], fac_b[:RANK].T, preferred_element_type=jnp.float32),
            jnp.dot(grad_rows[:, KEY_VALUE_WIDTH:], fac_b[RANK:].T, preferred_element_type=jnp.float32)], axis=1).astype(jnp.bfloat16)
        backward_partial = jnp.dot(low_rank_gradient, factor_down.T, preferred_element_type=jnp.float32)
        tile_down_gradient = adapter_scale * jnp.dot(token_rows.T, low_rank_gradient, preferred_element_type=jnp.float32)
        tile_up_gradient = adapter_scale * jnp.concatenate([
            jnp.dot(rank_act[:, :RANK].T, grad_rows[:, :KEY_VALUE_WIDTH], preferred_element_type=jnp.float32),
            jnp.dot(rank_act[:, RANK:].T, grad_rows[:, KEY_VALUE_WIDTH:], preferred_element_type=jnp.float32)], axis=0)
        return adapter_partial, backward_partial, tile_down_gradient, tile_up_gradient

    adapter_partial, backward_partial, tile_down_gradient, tile_up_gradient = lax.map(single_tile, (token_tile_index, gradient_per_tile, tile_index_list))
    base_product = jnp.dot(tokens, weight, preferred_element_type=jnp.float32)
    key_value_output = (base_product + adapter_scale * adapter_partial.reshape(overall_row_count, 2 * KEY_VALUE_WIDTH)).astype(jnp.bfloat16)
    backward_pass = jnp.dot(grad_out, weight.T, preferred_element_type=jnp.float32)
    token_gradient = (backward_pass + adapter_scale * backward_partial.reshape(overall_row_count, MODEL_WIDTH)).astype(jnp.bfloat16)
    grad_a = jax.ops.segment_sum(tile_down_gradient, tile_index_list, num_segments=ADAPTERS)
    grad_b = jax.ops.segment_sum(tile_up_gradient, tile_index_list, num_segments=ADAPTERS)
    return key_value_output, token_gradient, grad_a, grad_b
```

```python
import jax
import jax.numpy as jnp
from jax import lax
from jax.sharding import PartitionSpec as P

adapter_scale = 0.5
f32 = jnp.float32
bf16 = jnp.bfloat16


def swap(value, bit):
    count = lax.axis_size("blk")
    return lax.ppermute(value, "blk", [(i, i ^ (1 << bit)) for i in range(count)])


def dot(a, b, contract):
    return lax.dot_general(a, b, ((contract[:1], contract[1:]), ((), ())), preferred_element_type=f32)


def pick(blocks, hits):
    out = jnp.where(hits[0], blocks[0], jnp.zeros_like(blocks[0]))
    for block, hit in zip(blocks[1:], hits[1:]):
        out = jnp.where(hit, block, out)
    return out


def blend(blocks, hits):
    out = jnp.zeros(blocks[0].shape, f32)
    for block, hit in zip(blocks, hits):
        out = out + jnp.where(hit, block.astype(f32), 0.0)
    return out


def gather_high(own, high_bits):
    blocks = [own]
    for bit in high_bits:
        blocks = blocks + [swap(block, bit) for block in blocks]
    return blocks


def on_device(tokens, weight, bank_a, bank_b, tile_map, grad_out):
    blk_count = lax.axis_size("blk")
    tp_count = lax.axis_size("tp")
    me = lax.axis_index("blk")
    col = lax.axis_index("tp")
    bit_count = blk_count.bit_length() - 1
    core_bit, cross_bit = 0, 1
    high_bits = list(range(bit_count - 1, 1, -1))
    offsets = [0]
    for bit in high_bits:
        offsets = offsets + [o | (1 << bit) for o in offsets]
    both = offsets + [o | 1 for o in offsets]

    rows = tokens.shape[0]
    tile_count = tile_map.shape[0]
    tile_rows = rows // tile_count
    rank_two = bank_a.shape[2]
    rank_one = rank_two // 2
    kv_width = bank_b.shape[2]
    kv_dev = kv_width // tp_count
    local_rows = rows // tp_count

    own_a = bank_a[0].T
    own_b = bank_b[0]
    mine = [tile_map[k, 0] for k in range(tile_count)]
    map_far = swap(tile_map, cross_bit)
    theirs = [map_far[k, 0] for k in range(tile_count)]

    def gather(own):
        blocks = gather_high(own, high_bits)
        blocks = blocks + [swap(block, core_bit) for block in blocks]
        sent = [pick(blocks, [(m ^ me) == o for o in both]) for m in theirs]
        got = [swap(s, cross_bit) for s in sent]
        here = [pick(blocks, [(m ^ me) == o for o in both]) for m in mine]
        return [
            jnp.where(((m ^ me) & 2) == 0, h, g) for m, h, g in zip(mine, here, got)
        ]

    def give_back(parts):
        sent = [p.astype(bf16) for p in parts]
        got = [swap(s, cross_bit) for s in sent]
        held = list(parts) + got
        owner = mine + theirs
        away = [blend(held, [(m ^ me) == (o | 1) for m in owner]).astype(bf16) for o in offsets]
        keep = [blend(held, [(m ^ me) == o for m in owner]) for o in offsets]
        back = [swap(a, core_bit) for a in away]
        total = {o: k + b.astype(f32) for o, k, b in zip(offsets, keep, back)}
        for bit in reversed(high_bits):
            far = [o for o in total if o >> bit & 1]
            far.sort(reverse=True)
            came = {o: swap(total[o].astype(bf16), bit) for o in far}
            total = {o: total[o] + came[o | 1 << bit].astype(f32) for o in total if not o >> bit & 1}
        return total[0]

    if tp_count == 2:
        other = lax.ppermute(grad_out, "tp", [(0, 1), (1, 0)])
        grad_rows = jnp.where(
            col == 0,
            jnp.concatenate([grad_out, other], axis=0),
            jnp.concatenate([other, grad_out], axis=0),
        )
    else:
        grad_rows = lax.all_gather(grad_out, "tp", axis=0, tiled=True)

    factor_b = gather(own_b)
    zero = jnp.zeros((rank_one, kv_width), bf16)
    wide_b = [
        jnp.concatenate(
            [
                jnp.concatenate([b[:rank_one], zero], axis=1),
                jnp.concatenate([zero, b[rank_one:]], axis=1),
            ],
            axis=0,
        )
        for b in factor_b
    ]
    factor_a = gather(own_a)

    base = dot(tokens, weight, (1, 0))
    if tp_count == 2:
        far_base = lax.dynamic_slice_in_dim(base, (1 - col) * local_rows, local_rows, 0)
        near_base = lax.dynamic_slice_in_dim(base, col * local_rows, local_rows, 0)
        base_rows = near_base + lax.ppermute(far_base.astype(bf16), "tp", [(0, 1), (1, 0)]).astype(f32)
    else:
        base_rows = lax.psum_scatter(base, "tp", scatter_dimension=0, tiled=True)

    tiles = [tokens[k * tile_rows : (k + 1) * tile_rows] for k in range(tile_count)]
    grads = [grad_rows[k * tile_rows : (k + 1) * tile_rows] for k in range(tile_count)]

    rank_grad = [dot(b, g, (1, 1)).astype(bf16) for b, g in zip(wide_b, grads)]
    grad_a = give_back([adapter_scale * dot(r, x, (1, 0)) for r, x in zip(rank_grad, tiles)])

    rank_part = jnp.concatenate([dot(a, x, (1, 1)) for a, x in zip(factor_a, tiles)], axis=1)
    if tp_count == 2:
        rank_sum = rank_part + lax.ppermute(rank_part, "tp", [(0, 1), (1, 0)])
    else:
        rank_sum = lax.psum(rank_part, "tp")
    rank_act = rank_sum.astype(bf16)

    first = col * local_rows
    local_act = lax.dynamic_slice_in_dim(rank_act, first, local_rows, 1)
    local_b = pick(wide_b, [first // tile_rows == k for k in range(tile_count)])
    key_value_output = (base_rows + adapter_scale * dot(local_act, local_b, (0, 0))).astype(bf16)

    up = []
    for k in range(tile_count):
        whole = adapter_scale * dot(
            rank_act[:, k * tile_rows : (k + 1) * tile_rows], grads[k], (1, 0)
        )
        up.append(
            jnp.concatenate(
                [
                    lax.dynamic_slice(whole[:rank_one, :kv_width], (0, col * kv_dev), (rank_one, kv_dev)),
                    lax.dynamic_slice(whole[rank_one:, kv_width:], (0, col * kv_dev), (rank_one, kv_dev)),
                ],
                axis=0,
            )
        )
    grad_b = give_back(up)

    backward = dot(grad_rows, weight, (1, 1))
    lora = jnp.concatenate([dot(r, a, (0, 0)) for r, a in zip(rank_grad, factor_a)], axis=0)
    token_gradient = (backward + adapter_scale * lora).astype(bf16)
    return key_value_output, token_gradient, grad_a.T[None], grad_b[None]


def solution(mesh):
    in_specs = (
        P("blk", "tp"),
        P("tp", None),
        P("blk", "tp", None),
        P("blk", None, None),
        P("blk", None),
        P(("blk", "tp"), None),
    )
    out_specs = (P(("blk", "tp"), None), P("blk", "tp"), P("blk", "tp", None), P("blk", None, "tp"))
    return jax.shard_map(
        on_device, mesh=mesh, in_specs=in_specs, out_specs=out_specs, check_vma=False
    )
```

```python
import jax
import jax.numpy as jnp
from jax import lax
from jax.sharding import PartitionSpec as P

adapter_scale = 0.5
f32 = jnp.float32
bf16 = jnp.bfloat16
core, far = 1, 2


def swap(value, offset):
    count = lax.axis_size("blk")
    return lax.ppermute(value, "blk", [(i, i ^ offset) for i in range(count)])


def cross(value):
    return lax.ppermute(value, "tp", [(0, 1), (1, 0)])


def dot(a, b, contract):
    return lax.dot_general(a, b, ((contract[:1], contract[1:]), ((), ())), preferred_element_type=f32)


def pick(blocks, hits):
    out = jnp.where(hits[0], blocks[0], jnp.zeros_like(blocks[0]))
    for block, hit in zip(blocks[1:], hits[1:]):
        out = jnp.where(hit, block, out)
    return out


def blend(blocks, hits):
    out = jnp.zeros(blocks[0].shape, f32)
    for block, hit in zip(blocks, hits):
        out = out + jnp.where(hit, block.astype(f32), 0.0)
    return out


def after(value, *others):
    return lax.optimization_barrier((value,) + others)[0]


def plan(me, tile_map, map_far, places, rank):
    stacked = tile_map.shape[0] * rank
    shape = (stacked, len(places) * rank)
    tile, lane = lax.broadcasted_iota(jnp.int32, shape, 0), lax.broadcasted_iota(jnp.int32, shape, 1)
    same_row = tile % rank == lane % rank
    place = jnp.zeros(shape, jnp.int32)
    for i, o in enumerate(places):
        place = jnp.where(lane // rank == i, o, place)
    near, away = [
        jnp.broadcast_to((m ^ me)[:, :, None], (m.shape[0], rank, 1)).reshape(stacked, 1)
        for m in (tile_map, map_far)
    ]
    routes = [
        (same_row & (wanted == (place | side))).astype(bf16) for wanted in (near, away) for side in (0, core)
    ]
    square = (stacked, stacked)
    same = lax.broadcasted_iota(jnp.int32, square, 0) == lax.broadcasted_iota(jnp.int32, square, 1)
    return routes + [(same & ((near & far) != 0)).astype(bf16)]


def on_device(tokens, weight, bank_a, bank_b, tile_map, grad_out):
    blk_count = lax.axis_size("blk")
    tp_count = lax.axis_size("tp")
    me = lax.axis_index("blk")
    col = lax.axis_index("tp")
    offsets = list(range(0, blk_count, 4))
    bits = list(range(2, blk_count.bit_length() - 1))
    c_parts = 2

    rows = tokens.shape[0]
    features = tokens.shape[1]
    tile_count = tile_map.shape[0]
    tile_rows = rows // tile_count
    rank_two = bank_a.shape[2]
    rank_one = rank_two // 2
    kv_width = bank_b.shape[2]
    kv_dev = kv_width // tp_count
    local_rows = rows // tp_count
    stacked = tile_count * rank_two

    own_a = bank_a[0].T
    own_b = bank_b[0]
    map_far = swap(tile_map, far)
    keep = (
        lax.broadcasted_iota(jnp.int32, (stacked, rows), 0) // rank_two
        == lax.broadcasted_iota(jnp.int32, (stacked, rows), 1) // tile_rows
    )

    def split(value, count=rank_two):
        return [value[i : i + count] for i in range(0, value.shape[0], count)]

    places = [0]
    for bit in reversed(bits):
        places = places + [o | 1 << bit for o in places]

    def joined_hops(own):
        blocks, hops = own, []
        for bit in reversed(bits):
            more = swap(blocks, 1 << bit)
            hops.append(more)
            blocks = jnp.concatenate([blocks, more], axis=0)
        return blocks, hops

    def give_away(here, there):
        return (dot(far_here, here, (1, 0)) + dot(far_there, there, (1, 0))).astype(bf16)

    def take_in(here, there, got):
        return (
            dot(near_here, here, (1, 0)) + dot(near_there, there, (1, 0)) + dot(from_far, got, (1, 0))
        ).astype(bf16)

    def sums(sent, got, back):
        kept = dot(near_here, sent, (0, 0)) + dot(far_here, got, (0, 0)) + back.astype(f32)
        return dict(zip(places, split(kept)))

    def core_part(sent, got):
        return (dot(near_there, sent, (0, 0)) + dot(far_there, got, (0, 0))).astype(bf16)

    def leaving(total, bit):
        return jnp.concatenate([total[o].astype(bf16) for o in total if o >> bit & 1], axis=0)

    def add_hop(total, came, bit):
        gone = [o for o in total if o >> bit & 1]
        return {
            o ^ 1 << bit: total[o ^ 1 << bit] + c.astype(f32) for o, c in zip(gone, split(came))
        }

    if tp_count == 2:
        other = cross(grad_out)
        grad_rows = jnp.where(
            col == 0,
            jnp.concatenate([grad_out, other], axis=0),
            jnp.concatenate([other, grad_out], axis=0),
        )
    else:
        grad_rows = lax.all_gather(grad_out, "tp", axis=0, tiled=True)

    here_b, hops_b = joined_hops(own_b)
    near_here, near_there, far_here, far_there, from_far = plan(
        me, tile_map, after(map_far, hops_b[-1]), places, rank_two
    )
    there_b = swap(here_b, core)
    factor_b = take_in(here_b, there_b, swap(give_away(here_b, there_b), far))
    key_row = lax.broadcasted_iota(jnp.int32, factor_b.shape, 0) % rank_two < rank_one
    nothing = jnp.zeros_like(factor_b)
    wide_b = jnp.concatenate(
        [jnp.where(key_row, factor_b, nothing), jnp.where(key_row, nothing, factor_b)], axis=1
    )
    rank_grad = jnp.where(keep, dot(wide_b, grad_rows, (1, 1)), 0.0).astype(bf16)
    width_c = features // c_parts
    down = [
        (adapter_scale * dot(rank_grad, tokens[:, i * width_c : (i + 1) * width_c], (1, 0))).astype(bf16)
        for i in range(c_parts)
    ]

    blocks_a = [after(own_a, there_b)]
    late_hop = None
    for bit in reversed(bits):
        if len(blocks_a) > 1:
            blocks_a[-1] = late_hop = after(blocks_a[-1], down[0])
        blocks_a = blocks_a + [swap(block, 1 << bit) for block in blocks_a]
    here_a = jnp.concatenate(blocks_a, axis=0)
    if tp_count == 2:
        base = dot(after(tokens, late_hop), weight, (1, 0))
        near_base = lax.dynamic_slice_in_dim(base, col * local_rows, local_rows, 0)
        far_base = lax.dynamic_slice_in_dim(base, (1 - col) * local_rows, local_rows, 0).astype(bf16)
        base_rows = near_base + cross(far_base).astype(f32)
        here_a = after(here_a, far_base)
    else:
        far_base = dot(tokens, weight, (1, 0))
        base_rows = lax.psum_scatter(far_base, "tp", scatter_dimension=0, tiled=True)
    there_a = swap(here_a, core)
    sent_a = give_away(here_a, there_a)
    factor_a = take_in(here_a, there_a, swap(sent_a, far))

    got_c = [swap(d, far) for d in down]
    got_c[0] = after(got_c[0], here_a)
    back = swap(core_part(down[0], got_c[0]), core)
    total = sums(down[0], got_c[0], back)
    first_gone = after(leaving(total, bits[0]), sent_a)
    total = add_hop(total, swap(first_gone, 1 << bits[0]), bits[0])

    got_c[1] = after(got_c[1], first_gone)
    away = core_part(down[1], got_c[1])
    base_grad = dot(after(grad_rows, sent_a, away), weight, (1, 1))

    total_c = []
    first_came = None
    mark = base_grad
    for i in range(c_parts):
        if i:
            total = sums(down[i], got_c[i], swap(away, core))
            first_came = swap(after(leaving(total, bits[0]), mark), 1 << bits[0])
            total = add_hop(total, first_came, bits[0])
        for bit in bits[1:]:
            mark = after(leaving(total, bit), mark)
            total = add_hop(total, swap(mark, 1 << bit), bit)
        total_c.append(total)
    grad_a = jnp.concatenate([total[0] for total in total_c], axis=1)

    rank_part = jnp.where(keep, dot(factor_a, tokens, (1, 1)), 0.0)
    rank_part = sum(split(rank_part))
    if tp_count == 2:
        rank_sum = rank_part + cross(rank_part)
    else:
        rank_sum = lax.psum(rank_part, "tp")
    rank_act = rank_sum.astype(bf16)

    first = col * local_rows
    local_act = lax.dynamic_slice_in_dim(rank_act, first, local_rows, 1)
    local_b = pick(split(wide_b), [first // tile_rows == k for k in range(tile_count)])
    key_value_output = (base_rows + adapter_scale * dot(local_act, local_b, (0, 0))).astype(bf16)

    spread = jnp.where(keep, jnp.concatenate([rank_act] * tile_count, axis=0), jnp.zeros((), bf16))
    whole = adapter_scale * dot(spread, grad_rows, (1, 0))
    key_part = lax.dynamic_slice(whole, (0, col * kv_dev), (stacked, kv_dev))
    value_part = lax.dynamic_slice(whole, (0, kv_width + col * kv_dev), (stacked, kv_dev))
    up = jnp.where(key_row[:, :kv_dev], key_part, value_part).astype(bf16)
    got_up = after(swap(up, far), first_came)
    back_up = swap(core_part(up, got_up), core)
    total_up = sums(up, got_up, back_up)
    leave = [after(total_up[o].astype(bf16), mark) for o in places[1:]]
    came_up = [swap(t, o) for o, t in zip(places[1:], leave)]
    grad_b = sum([c.astype(f32) for c in came_up], total_up[0])

    lora_grad = dot(after(rank_grad, rank_act), factor_a, (0, 0))
    token_gradient = (after(base_grad, rank_act) + adapter_scale * lora_grad).astype(bf16)
    return key_value_output, token_gradient, grad_a.T[None], grad_b[None]


def solution(mesh):
    in_specs = (
        P("blk", "tp"),
        P("tp", None),
        P("blk", "tp", None),
        P("blk", None, None),
        P("blk", None),
        P(("blk", "tp"), None),
    )
    out_specs = (P(("blk", "tp"), None), P("blk", "tp"), P("blk", "tp", None), P("blk", None, "tp"))
    return jax.shard_map(
        on_device, mesh=mesh, in_specs=in_specs, out_specs=out_specs, check_vma=False
    )
```

```python
import jax
import jax.numpy as jnp
from jax import lax
from jax.sharding import PartitionSpec as P

adapter_scale = 0.5
f32 = jnp.float32
bf16 = jnp.bfloat16
core, far = 1, 2


def swap(value, offset):
    count = lax.axis_size("blk")
    return lax.ppermute(value, "blk", [(i, i ^ offset) for i in range(count)])


def cross(value):
    return lax.ppermute(value, "tp", [(0, 1), (1, 0)])


def dot(a, b, contract):
    return lax.dot_general(a, b, ((contract[:1], contract[1:]), ((), ())), preferred_element_type=f32)


def pick(blocks, hits):
    out = jnp.where(hits[0], blocks[0], jnp.zeros_like(blocks[0]))
    for block, hit in zip(blocks[1:], hits[1:]):
        out = jnp.where(hit, block, out)
    return out


def blend(blocks, hits):
    out = jnp.zeros(blocks[0].shape, f32)
    for block, hit in zip(blocks, hits):
        out = out + jnp.where(hit, block.astype(f32), 0.0)
    return out


def after(value, *others):
    return lax.optimization_barrier((value,) + others)[0]


def plan(me, tile_map, map_far, places, rank):
    stacked = tile_map.shape[0] * rank
    shape = (stacked, len(places) * rank)
    tile, lane = lax.broadcasted_iota(jnp.int32, shape, 0), lax.broadcasted_iota(jnp.int32, shape, 1)
    same_row = tile % rank == lane % rank
    place = jnp.zeros(shape, jnp.int32)
    for i, o in enumerate(places):
        place = jnp.where(lane // rank == i, o, place)
    near, away = [
        jnp.broadcast_to((m ^ me)[:, :, None], (m.shape[0], rank, 1)).reshape(stacked, 1)
        for m in (tile_map, map_far)
    ]
    routes = [
        (same_row & (wanted == (place | side))).astype(bf16) for wanted in (near, away) for side in (0, core)
    ]
    square = (stacked, stacked)
    same = lax.broadcasted_iota(jnp.int32, square, 0) == lax.broadcasted_iota(jnp.int32, square, 1)
    return routes + [(same & ((near & far) != 0)).astype(bf16)]


def on_device(tokens, weight, bank_a, bank_b, tile_map, grad_out):
    blk_count = lax.axis_size("blk")
    tp_count = lax.axis_size("tp")
    me = lax.axis_index("blk")
    col = lax.axis_index("tp")
    offsets = list(range(0, blk_count, 4))
    bits = list(range(2, blk_count.bit_length() - 1))
    c_parts = 2

    rows = tokens.shape[0]
    features = tokens.shape[1]
    tile_count = tile_map.shape[0]
    tile_rows = rows // tile_count
    rank_two = bank_a.shape[2]
    rank_one = rank_two // 2
    kv_width = bank_b.shape[2]
    kv_dev = kv_width // tp_count
    local_rows = rows // tp_count
    stacked = tile_count * rank_two

    own_a = bank_a[0].T
    own_b = bank_b[0]
    map_far = swap(tile_map, far)
    keep = (
        lax.broadcasted_iota(jnp.int32, (stacked, rows), 0) // rank_two
        == lax.broadcasted_iota(jnp.int32, (stacked, rows), 1) // tile_rows
    )

    def split(value, count=rank_two):
        return [value[i : i + count] for i in range(0, value.shape[0], count)]

    places = [0]
    for bit in reversed(bits):
        places = places + [o | 1 << bit for o in places]

    def joined_hops(own):
        blocks, hops = own, []
        for bit in reversed(bits):
            more = swap(blocks, 1 << bit)
            hops.append(more)
            blocks = jnp.concatenate([blocks, more], axis=0)
        return blocks, hops

    def give_away(here, there):
        return (dot(far_here, here, (1, 0)) + dot(far_there, there, (1, 0))).astype(bf16)

    def take_in(here, there, got):
        return (
            dot(near_here, here, (1, 0)) + dot(near_there, there, (1, 0)) + dot(from_far, got, (1, 0))
        ).astype(bf16)

    def sums(sent, got, back):
        kept = dot(near_here, sent, (0, 0)) + dot(far_here, got, (0, 0)) + back.astype(f32)
        return dict(zip(places, split(kept)))

    def core_part(sent, got):
        return (dot(near_there, sent, (0, 0)) + dot(far_there, got, (0, 0))).astype(bf16)

    def leaving(total, bit):
        return jnp.concatenate([total[o].astype(bf16) for o in total if o >> bit & 1], axis=0)

    def add_hop(total, came, bit):
        gone = [o for o in total if o >> bit & 1]
        return {
            o ^ 1 << bit: total[o ^ 1 << bit] + c.astype(f32) for o, c in zip(gone, split(came))
        }

    if tp_count == 2:
        other = cross(grad_out)
        grad_rows = jnp.where(
            col == 0,
            jnp.concatenate([grad_out, other], axis=0),
            jnp.concatenate([other, grad_out], axis=0),
        )
    else:
        grad_rows = lax.all_gather(grad_out, "tp", axis=0, tiled=True)

    here_b, hops_b = joined_hops(own_b)
    near_here, near_there, far_here, far_there, from_far = plan(
        me, after(tile_map, hops_b[0]), after(map_far, hops_b[0]), places, rank_two
    )
    there_b = swap(here_b, core)
    sent_b = give_away(here_b, there_b)
    factor_b = take_in(here_b, there_b, swap(sent_b, far))
    key_row = lax.broadcasted_iota(jnp.int32, factor_b.shape, 0) % rank_two < rank_one
    nothing = jnp.zeros_like(factor_b)
    wide_b = jnp.concatenate(
        [jnp.where(key_row, factor_b, nothing), jnp.where(key_row, nothing, factor_b)], axis=1
    )
    rank_grad = jnp.where(keep, dot(wide_b, grad_rows, (1, 1)), 0.0).astype(bf16)
    width_c = features // c_parts
    down = [
        (adapter_scale * dot(rank_grad, tokens[:, i * width_c : (i + 1) * width_c], (1, 0))).astype(bf16)
        for i in range(c_parts)
    ]

    blocks_a = [after(own_a, sent_b)]
    late_hop = None
    for bit in reversed(bits):
        if len(blocks_a) > 1:
            blocks_a[-1] = late_hop = after(blocks_a[-1], down[0])
        blocks_a = blocks_a + [swap(block, 1 << bit) for block in blocks_a]
    here_a = jnp.concatenate(blocks_a, axis=0)
    if tp_count == 2:
        base = dot(after(tokens, late_hop), weight, (1, 0))
        near_base = lax.dynamic_slice_in_dim(base, col * local_rows, local_rows, 0)
        far_base = lax.dynamic_slice_in_dim(base, (1 - col) * local_rows, local_rows, 0).astype(bf16)
        base_rows = near_base + cross(far_base).astype(f32)
        here_a = after(here_a, far_base)
    else:
        far_base = dot(tokens, weight, (1, 0))
        base_rows = lax.psum_scatter(far_base, "tp", scatter_dimension=0, tiled=True)
    there_a = swap(here_a, core)
    sent_a = give_away(here_a, there_a)

    got_c = [swap(d, far) for d in down]
    got_c[0] = after(got_c[0], here_a)
    back = after(swap(core_part(down[0], got_c[0]), core), sent_a)
    total = sums(down[0], got_c[0], back)
    first_gone = after(leaving(total, bits[0]), sent_a)
    total = add_hop(total, swap(first_gone, 1 << bits[0]), bits[0])

    got_c[1] = after(got_c[1], first_gone)
    away = core_part(down[1], got_c[1])
    base_grad = dot(after(grad_rows, sent_a, away), weight, (1, 1))

    factor_a = take_in(here_a, there_a, after(swap(sent_a, far), base_grad))
    rank_part = jnp.where(keep, dot(factor_a, tokens, (1, 1)), 0.0)
    rank_part = sum(split(rank_part))

    total_c = []
    first_came = None
    mark = rank_part
    for i in range(c_parts):
        if i:
            total = sums(down[i], got_c[i], swap(away, core))
            first_came = swap(after(leaving(total, bits[0]), mark), 1 << bits[0])
            total = add_hop(total, first_came, bits[0])
        for bit in bits[1:]:
            mark = after(leaving(total, bit), mark)
            total = add_hop(total, swap(mark, 1 << bit), bit)
        total_c.append(total)
    grad_a = jnp.concatenate([total[0] for total in total_c], axis=1)

    if tp_count == 2:
        rank_sum = rank_part + cross(rank_part)
    else:
        rank_sum = lax.psum(rank_part, "tp")
    rank_act = rank_sum.astype(bf16)

    first = col * local_rows
    local_act = lax.dynamic_slice_in_dim(rank_act, first, local_rows, 1)
    local_b = pick(split(wide_b), [first // tile_rows == k for k in range(tile_count)])
    key_value_output = (base_rows + adapter_scale * dot(local_act, local_b, (0, 0))).astype(bf16)

    spread = jnp.where(keep, jnp.concatenate([rank_act] * tile_count, axis=0), jnp.zeros((), bf16))
    whole = adapter_scale * dot(spread, grad_rows, (1, 0))
    key_part = lax.dynamic_slice(whole, (0, col * kv_dev), (stacked, kv_dev))
    value_part = lax.dynamic_slice(whole, (0, kv_width + col * kv_dev), (stacked, kv_dev))
    up = jnp.where(key_row[:, :kv_dev], key_part, value_part).astype(bf16)
    got_up = after(swap(up, far), first_came)
    back_up = swap(core_part(up, got_up), core)
    total_up = sums(up, got_up, back_up)
    leave = [after(total_up[o].astype(bf16), mark) for o in places[1:]]
    came_up = [swap(t, o) for o, t in zip(places[1:], leave)]
    grad_b = sum([c.astype(f32) for c in came_up], total_up[0])

    lora_grad = dot(after(rank_grad, rank_act), factor_a, (0, 0))
    token_gradient = (after(base_grad, rank_act) + adapter_scale * lora_grad).astype(bf16)
    return key_value_output, token_gradient, grad_a.T[None], grad_b[None]


def solution(mesh):
    in_specs = (
        P("blk", "tp"),
        P("tp", None),
        P("blk", "tp", None),
        P("blk", None, None),
        P("blk", None),
        P(("blk", "tp"), None),
    )
    out_specs = (P(("blk", "tp"), None), P("blk", "tp"), P("blk", "tp", None), P("blk", None, "tp"))
    return jax.shard_map(
        on_device, mesh=mesh, in_specs=in_specs, out_specs=out_specs, check_vma=False
    )
```

```python
import jax
import jax.numpy as jnp
from jax import lax
from jax.sharding import PartitionSpec as P

adapter_scale = 0.5
f32 = jnp.float32
bf16 = jnp.bfloat16
core, far = 1, 2


def swap(value, offset):
    count = lax.axis_size("blk")
    return lax.ppermute(value, "blk", [(i, i ^ offset) for i in range(count)])


def cross(value):
    return lax.ppermute(value, "tp", [(0, 1), (1, 0)])


def dot(a, b, contract):
    return lax.dot_general(a, b, ((contract[:1], contract[1:]), ((), ())), preferred_element_type=f32)


def pick(blocks, hits):
    out = jnp.where(hits[0], blocks[0], jnp.zeros_like(blocks[0]))
    for block, hit in zip(blocks[1:], hits[1:]):
        out = jnp.where(hit, block, out)
    return out


def blend(blocks, hits):
    out = jnp.zeros(blocks[0].shape, f32)
    for block, hit in zip(blocks, hits):
        out = out + jnp.where(hit, block.astype(f32), 0.0)
    return out


def after(value, *others):
    return lax.optimization_barrier((value,) + others)[0]


def plan(me, tile_map, map_far, places, rank):
    stacked = tile_map.shape[0] * rank
    shape = (stacked, len(places) * rank)
    tile, lane = lax.broadcasted_iota(jnp.int32, shape, 0), lax.broadcasted_iota(jnp.int32, shape, 1)
    same_row = tile % rank == lane % rank
    place = jnp.zeros(shape, jnp.int32)
    for i, o in enumerate(places):
        place = jnp.where(lane // rank == i, o, place)
    near, away = [
        jnp.broadcast_to((m ^ me)[:, :, None], (m.shape[0], rank, 1)).reshape(stacked, 1)
        for m in (tile_map, map_far)
    ]
    routes = [
        (same_row & (wanted == (place | side))).astype(bf16) for wanted in (near, away) for side in (0, core)
    ]
    square = (stacked, stacked)
    same = lax.broadcasted_iota(jnp.int32, square, 0) == lax.broadcasted_iota(jnp.int32, square, 1)
    return routes + [(same & ((near & far) != 0)).astype(bf16)]


def on_device(tokens, weight, bank_a, bank_b, tile_map, grad_out):
    blk_count = lax.axis_size("blk")
    tp_count = lax.axis_size("tp")
    me = lax.axis_index("blk")
    col = lax.axis_index("tp")
    offsets = list(range(0, blk_count, 4))
    bits = list(range(2, blk_count.bit_length() - 1))
    c_parts = 2

    rows = tokens.shape[0]
    features = tokens.shape[1]
    tile_count = tile_map.shape[0]
    tile_rows = rows // tile_count
    rank_two = bank_a.shape[2]
    rank_one = rank_two // 2
    kv_width = bank_b.shape[2]
    kv_dev = kv_width // tp_count
    local_rows = rows // tp_count
    stacked = tile_count * rank_two

    own_a = bank_a[0].T
    own_b = bank_b[0]
    map_far = swap(tile_map, far)
    keep = (
        lax.broadcasted_iota(jnp.int32, (stacked, rows), 0) // rank_two
        == lax.broadcasted_iota(jnp.int32, (stacked, rows), 1) // tile_rows
    )

    def split(value, count=rank_two):
        return [value[i : i + count] for i in range(0, value.shape[0], count)]

    places = [0]
    for bit in reversed(bits):
        places = places + [o | 1 << bit for o in places]

    def joined_hops(own):
        blocks, hops = own, []
        for bit in reversed(bits):
            more = swap(blocks, 1 << bit)
            hops.append(more)
            blocks = jnp.concatenate([blocks, more], axis=0)
        return blocks, hops

    def give_away(here, there):
        return (dot(far_here, here, (1, 0)) + dot(far_there, there, (1, 0))).astype(bf16)

    def take_in(here, there, got):
        return (
            dot(near_here, here, (1, 0)) + dot(near_there, there, (1, 0)) + dot(from_far, got, (1, 0))
        ).astype(bf16)

    def sums(sent, got, back):
        kept = dot(near_here, sent, (0, 0)) + dot(far_here, got, (0, 0)) + back.astype(f32)
        return dict(zip(places, split(kept)))

    def core_part(sent, got):
        return (dot(near_there, sent, (0, 0)) + dot(far_there, got, (0, 0))).astype(bf16)

    def leaving(total, bit):
        return jnp.concatenate([total[o].astype(bf16) for o in total if o >> bit & 1], axis=0)

    def add_hop(total, came, bit):
        gone = [o for o in total if o >> bit & 1]
        return {
            o ^ 1 << bit: total[o ^ 1 << bit] + c.astype(f32) for o, c in zip(gone, split(came))
        }

    if tp_count == 2:
        other = cross(grad_out)
        grad_rows = jnp.where(
            col == 0,
            jnp.concatenate([grad_out, other], axis=0),
            jnp.concatenate([other, grad_out], axis=0),
        )
    else:
        grad_rows = lax.all_gather(grad_out, "tp", axis=0, tiled=True)

    here_b, hops_b = joined_hops(own_b)
    near_here, near_there, far_here, far_there, from_far = plan(
        me, after(tile_map, hops_b[0]), after(map_far, hops_b[0]), places, rank_two
    )
    there_b = swap(here_b, core)
    sent_b = give_away(here_b, there_b)
    factor_b = take_in(here_b, there_b, swap(sent_b, far))
    key_row = lax.broadcasted_iota(jnp.int32, factor_b.shape, 0) % rank_two < rank_one
    nothing = jnp.zeros_like(factor_b)
    wide_b = jnp.concatenate(
        [jnp.where(key_row, factor_b, nothing), jnp.where(key_row, nothing, factor_b)], axis=1
    )
    rank_grad = jnp.where(keep, dot(wide_b, grad_rows, (1, 1)), 0.0).astype(bf16)
    width_c = features // c_parts
    down = [
        (adapter_scale * dot(rank_grad, tokens[:, i * width_c : (i + 1) * width_c], (1, 0))).astype(bf16)
        for i in range(c_parts)
    ]

    blocks_a = [after(own_a, sent_b)]
    late_hop = None
    for bit in reversed(bits):
        if len(blocks_a) > 1:
            blocks_a[-1] = late_hop = after(blocks_a[-1], down[0])
        blocks_a = blocks_a + [swap(block, 1 << bit) for block in blocks_a]
    here_a = jnp.concatenate(blocks_a, axis=0)
    if tp_count == 2:
        base = dot(after(tokens, sent_b), weight, (1, 0))
        near_base = lax.dynamic_slice_in_dim(base, col * local_rows, local_rows, 0)
        far_base = lax.dynamic_slice_in_dim(base, (1 - col) * local_rows, local_rows, 0).astype(bf16)
        base_rows = near_base + cross(far_base).astype(f32)
    else:
        far_base = dot(tokens, weight, (1, 0))
        base_rows = lax.psum_scatter(far_base, "tp", scatter_dimension=0, tiled=True)
    half = features // 2
    base_low = dot(after(grad_rows, late_hop), weight[:half], (1, 1))
    here_a = after(here_a, base_low)
    there_a = swap(here_a, core)
    sent_a = give_away(here_a, there_a)

    got_c = [swap(d, far) for d in down]
    got_c[0] = after(got_c[0], here_a)
    back = after(swap(core_part(down[0], got_c[0]), core), sent_a)
    total = sums(down[0], got_c[0], back)
    first_gone = after(leaving(total, bits[0]), sent_a)
    total = add_hop(total, swap(first_gone, 1 << bits[0]), bits[0])

    got_c[1] = after(got_c[1], first_gone)
    away = core_part(down[1], got_c[1])
    base_high = dot(after(grad_rows, sent_a, away), weight[half:], (1, 1))

    factor_a = take_in(here_a, there_a, after(swap(sent_a, far), base_high))
    rank_part = jnp.where(keep, dot(factor_a, tokens, (1, 1)), 0.0)
    rank_part = sum(split(rank_part))

    total_c = []
    first_came = None
    mark = rank_part
    for i in range(c_parts):
        if i:
            total = sums(down[i], got_c[i], swap(away, core))
            first_came = swap(after(leaving(total, bits[0]), mark), 1 << bits[0])
            total = add_hop(total, first_came, bits[0])
        for bit in bits[1:]:
            mark = after(leaving(total, bit), mark)
            total = add_hop(total, swap(mark, 1 << bit), bit)
        total_c.append(total)
    grad_a = jnp.concatenate([total[0] for total in total_c], axis=1)

    if tp_count == 2:
        rank_sum = rank_part + cross(rank_part)
    else:
        rank_sum = lax.psum(rank_part, "tp")
    rank_act = rank_sum.astype(bf16)

    first = col * local_rows
    local_act = lax.dynamic_slice_in_dim(rank_act, first, local_rows, 1)
    local_b = pick(split(wide_b), [first // tile_rows == k for k in range(tile_count)])
    key_value_output = (base_rows + adapter_scale * dot(local_act, local_b, (0, 0))).astype(bf16)

    spread = jnp.where(keep, jnp.concatenate([rank_act] * tile_count, axis=0), jnp.zeros((), bf16))
    whole = adapter_scale * dot(spread, grad_rows, (1, 0))
    key_part = lax.dynamic_slice(whole, (0, col * kv_dev), (stacked, kv_dev))
    value_part = lax.dynamic_slice(whole, (0, kv_width + col * kv_dev), (stacked, kv_dev))
    up = jnp.where(key_row[:, :kv_dev], key_part, value_part).astype(bf16)
    got_up = after(swap(up, far), first_came)
    back_up = swap(core_part(up, got_up), core)
    total_up = sums(up, got_up, back_up)
    leave = [after(total_up[o].astype(bf16), mark) for o in places[1:]]
    came_up = [swap(t, o) for o, t in zip(places[1:], leave)]
    grad_b = sum([c.astype(f32) for c in came_up], total_up[0])

    late_grad = after(rank_grad, rank_act)
    token_gradient = jnp.concatenate(
        [
            (after(base, rank_act) + adapter_scale * dot(late_grad, factor, (0, 0))).astype(bf16)
            for base, factor in ((base_low, factor_a[:, :half]), (base_high, factor_a[:, half:]))
        ],
        axis=1,
    )
    return key_value_output, token_gradient, grad_a.T[None], grad_b[None]


def solution(mesh):
    in_specs = (
        P("blk", "tp"),
        P("tp", None),
        P("blk", "tp", None),
        P("blk", None, None),
        P("blk", None),
        P(("blk", "tp"), None),
    )
    out_specs = (P(("blk", "tp"), None), P("blk", "tp"), P("blk", "tp", None), P("blk", None, "tp"))
    return jax.shard_map(
        on_device, mesh=mesh, in_specs=in_specs, out_specs=out_specs, check_vma=False
    )
```

```python
import jax
import jax.numpy as jnp
from jax import lax
from jax.sharding import PartitionSpec as P

adapter_scale = 0.5
f32 = jnp.float32
bf16 = jnp.bfloat16
core, far = 1, 2


def swap(value, offset):
    count = lax.axis_size("blk")
    return lax.ppermute(value, "blk", [(i, i ^ offset) for i in range(count)])


def cross(value):
    return lax.ppermute(value, "tp", [(0, 1), (1, 0)])


def dot(a, b, contract):
    return lax.dot_general(a, b, ((contract[:1], contract[1:]), ((), ())), preferred_element_type=f32)


def pick(blocks, hits):
    out = jnp.where(hits[0], blocks[0], jnp.zeros_like(blocks[0]))
    for block, hit in zip(blocks[1:], hits[1:]):
        out = jnp.where(hit, block, out)
    return out


def blend(blocks, hits):
    out = jnp.zeros(blocks[0].shape, f32)
    for block, hit in zip(blocks, hits):
        out = out + jnp.where(hit, block.astype(f32), 0.0)
    return out


def after(value, *others):
    return lax.optimization_barrier((value,) + others)[0]


def plan(me, tile_map, map_far, places, rank):
    stacked = tile_map.shape[0] * rank
    shape = (stacked, len(places) * rank)
    tile, lane = lax.broadcasted_iota(jnp.int32, shape, 0), lax.broadcasted_iota(jnp.int32, shape, 1)
    same_row = tile % rank == lane % rank
    place = jnp.zeros(shape, jnp.int32)
    for i, o in enumerate(places):
        place = jnp.where(lane // rank == i, o, place)
    near, away = [
        jnp.broadcast_to((m ^ me)[:, :, None], (m.shape[0], rank, 1)).reshape(stacked, 1)
        for m in (tile_map, map_far)
    ]
    routes = [
        (same_row & (wanted == (place | side))).astype(bf16) for wanted in (near, away) for side in (0, core)
    ]
    square = (stacked, stacked)
    same = lax.broadcasted_iota(jnp.int32, square, 0) == lax.broadcasted_iota(jnp.int32, square, 1)
    return routes + [(same & ((near & far) != 0)).astype(bf16)]


def on_device(tokens, weight, bank_a, bank_b, tile_map, grad_out):
    blk_count = lax.axis_size("blk")
    tp_count = lax.axis_size("tp")
    me = lax.axis_index("blk")
    col = lax.axis_index("tp")
    offsets = list(range(0, blk_count, 4))
    bits = list(range(2, blk_count.bit_length() - 1))
    c_parts = 2

    rows = tokens.shape[0]
    features = tokens.shape[1]
    tile_count = tile_map.shape[0]
    tile_rows = rows // tile_count
    rank_two = bank_a.shape[2]
    rank_one = rank_two // 2
    kv_width = bank_b.shape[2]
    kv_dev = kv_width // tp_count
    local_rows = rows // tp_count
    stacked = tile_count * rank_two

    own_a = bank_a[0].T
    own_b = bank_b[0]
    map_far = swap(tile_map, far)
    keep = (
        lax.broadcasted_iota(jnp.int32, (stacked, rows), 0) // rank_two
        == lax.broadcasted_iota(jnp.int32, (stacked, rows), 1) // tile_rows
    )

    def split(value, count=rank_two):
        return [value[i : i + count] for i in range(0, value.shape[0], count)]

    places = [0]
    for bit in reversed(bits):
        places = places + [o | 1 << bit for o in places]

    def joined_hops(own):
        blocks, hops = own, []
        for bit in reversed(bits):
            more = swap(blocks, 1 << bit)
            hops.append(more)
            blocks = jnp.concatenate([blocks, more], axis=0)
        return blocks, hops

    def give_away(here, there):
        return (dot(far_here, here, (1, 0)) + dot(far_there, there, (1, 0))).astype(bf16)

    def take_in(here, there, got):
        return (
            dot(near_here, here, (1, 0)) + dot(near_there, there, (1, 0)) + dot(from_far, got, (1, 0))
        ).astype(bf16)

    def sums(sent, got, back):
        kept = dot(near_here, sent, (0, 0)) + dot(far_here, got, (0, 0)) + back.astype(f32)
        return dict(zip(places, split(kept)))

    def core_part(sent, got):
        return (dot(near_there, sent, (0, 0)) + dot(far_there, got, (0, 0))).astype(bf16)

    def leaving(total, bit):
        return jnp.concatenate([total[o].astype(bf16) for o in total if o >> bit & 1], axis=0)

    def add_hop(total, came, bit):
        gone = [o for o in total if o >> bit & 1]
        return {
            o ^ 1 << bit: total[o ^ 1 << bit] + c.astype(f32) for o, c in zip(gone, split(came))
        }

    if tp_count == 2:
        other = cross(grad_out)
        grad_rows = jnp.where(
            col == 0,
            jnp.concatenate([grad_out, other], axis=0),
            jnp.concatenate([other, grad_out], axis=0),
        )
    else:
        grad_rows = lax.all_gather(grad_out, "tp", axis=0, tiled=True)

    here_b, hops_b = joined_hops(own_b)
    near_here, near_there, far_here, far_there, from_far = plan(
        me, after(tile_map, hops_b[0]), after(map_far, hops_b[0]), places, rank_two
    )
    there_b = swap(here_b, core)
    sent_b = give_away(here_b, there_b)
    factor_b = take_in(here_b, there_b, swap(sent_b, far))
    key_row = lax.broadcasted_iota(jnp.int32, factor_b.shape, 0) % rank_two < rank_one
    nothing = jnp.zeros_like(factor_b)
    wide_b = jnp.concatenate(
        [jnp.where(key_row, factor_b, nothing), jnp.where(key_row, nothing, factor_b)], axis=1
    )
    rank_grad = jnp.where(keep, dot(wide_b, grad_rows, (1, 1)), 0.0).astype(bf16)
    width_c = features // c_parts
    down = [
        (adapter_scale * dot(rank_grad, tokens[:, i * width_c : (i + 1) * width_c], (1, 0))).astype(bf16)
        for i in range(c_parts)
    ]

    blocks_a = [after(own_a, sent_b)]
    late_hop = None
    for bit in reversed(bits):
        if len(blocks_a) > 1:
            blocks_a[-1] = late_hop = after(blocks_a[-1], down[0])
        blocks_a = blocks_a + [swap(block, 1 << bit) for block in blocks_a]
    here_a = jnp.concatenate(blocks_a, axis=0)
    if tp_count == 2:
        base = dot(after(tokens, down[-1]), weight, (1, 0))
        near_base = lax.dynamic_slice_in_dim(base, col * local_rows, local_rows, 0)
        far_base = lax.dynamic_slice_in_dim(base, (1 - col) * local_rows, local_rows, 0).astype(bf16)
        base_rows = near_base + cross(far_base).astype(f32)
    else:
        far_base = dot(tokens, weight, (1, 0))
        base_rows = lax.psum_scatter(far_base, "tp", scatter_dimension=0, tiled=True)
    half = features // 2
    base_low = dot(after(grad_rows, late_hop), weight[:half], (1, 1))
    here_a = after(here_a, base_low)
    there_a = swap(here_a, core)
    sent_a = give_away(here_a, there_a)

    got_c = [after(swap(d, far), far_base) for d in down]
    back_c = [swap(core_part(d, g), core) for d, g in zip(down, got_c)]
    mark = sent_a
    total_c, came_c = [], []
    for sent, got, back in zip(down, got_c, back_c):
        total = sums(sent, got, after(back, sent_a))
        mark = after(leaving(total, bits[0]), mark)
        came_c.append(swap(mark, 1 << bits[0]))
        total_c.append(total)
    base_high = dot(after(grad_rows, mark), weight[half:], (1, 1))

    factor_a = take_in(here_a, there_a, after(swap(sent_a, far), base_high))
    rank_part = jnp.where(keep, dot(factor_a, tokens, (1, 1)), 0.0)
    rank_part = sum(split(rank_part))

    mark = rank_part
    ends = []
    for i, came in enumerate(came_c):
        total = add_hop(total_c[i], came, bits[0])
        for bit in bits[1:]:
            mark = after(leaving(total, bit), mark)
            came = swap(mark, 1 << bit)
            if bit == bits[-1]:
                ends.append((total, came))
            total = add_hop(total, came, bit)

    if tp_count == 2:
        rank_sum = rank_part + cross(rank_part)
    else:
        rank_sum = lax.psum(rank_part, "tp")
    rank_act = rank_sum.astype(bf16)

    first = col * local_rows
    local_act = lax.dynamic_slice_in_dim(rank_act, first, local_rows, 1)
    local_b = pick(split(wide_b), [first // tile_rows == k for k in range(tile_count)])
    key_value_output = (base_rows + adapter_scale * dot(local_act, local_b, (0, 0))).astype(bf16)

    spread = jnp.where(keep, jnp.concatenate([rank_act] * tile_count, axis=0), jnp.zeros((), bf16))
    whole = adapter_scale * dot(spread, grad_rows, (1, 0))
    key_part = lax.dynamic_slice(whole, (0, col * kv_dev), (stacked, kv_dev))
    value_part = lax.dynamic_slice(whole, (0, kv_width + col * kv_dev), (stacked, kv_dev))
    up = jnp.where(key_row[:, :kv_dev], key_part, value_part).astype(bf16)
    got_up = after(swap(up, far), mark)
    back_up = swap(core_part(up, got_up), core)
    total_up = sums(up, got_up, back_up)
    leave = [total_up[o].astype(bf16) for o in places[1:]]
    came_up = [swap(t, o) for o, t in zip(places[1:], leave)]
    grad_b = sum([c.astype(f32) for c in came_up], total_up[0])
    grad_a = jnp.concatenate(
        [add_hop(total, after(came, came_up[0]), bits[-1])[0] for total, came in ends], axis=1
    )

    late_grad = after(rank_grad, rank_act)
    token_gradient = jnp.concatenate(
        [
            (after(base, rank_act) + adapter_scale * dot(late_grad, factor, (0, 0))).astype(bf16)
            for base, factor in ((base_low, factor_a[:, :half]), (base_high, factor_a[:, half:]))
        ],
        axis=1,
    )
    return key_value_output, token_gradient, grad_a.T[None], grad_b[None]


def solution(mesh):
    in_specs = (
        P("blk", "tp"),
        P("tp", None),
        P("blk", "tp", None),
        P("blk", None, None),
        P("blk", None),
        P(("blk", "tp"), None),
    )
    out_specs = (P(("blk", "tp"), None), P("blk", "tp"), P("blk", "tp", None), P("blk", None, "tp"))
    return jax.shard_map(
        on_device, mesh=mesh, in_specs=in_specs, out_specs=out_specs, check_vma=False
    )
```

```python
import jax
import jax.numpy as jnp
from jax import lax
from jax.sharding import PartitionSpec as P

adapter_scale = 0.5
f32 = jnp.float32
bf16 = jnp.bfloat16
core, far = 1, 2


def swap(value, offset):
    count = lax.axis_size("blk")
    return lax.ppermute(value, "blk", [(i, i ^ offset) for i in range(count)])


def cross(value):
    return lax.ppermute(value, "tp", [(0, 1), (1, 0)])


def dot(a, b, contract):
    return lax.dot_general(a, b, ((contract[:1], contract[1:]), ((), ())), preferred_element_type=f32)


def pick(blocks, hits):
    out = jnp.where(hits[0], blocks[0], jnp.zeros_like(blocks[0]))
    for block, hit in zip(blocks[1:], hits[1:]):
        out = jnp.where(hit, block, out)
    return out


def blend(blocks, hits):
    out = jnp.zeros(blocks[0].shape, f32)
    for block, hit in zip(blocks, hits):
        out = out + jnp.where(hit, block.astype(f32), 0.0)
    return out


def after(value, *others):
    return lax.optimization_barrier((value,) + others)[0]


def plan(me, tile_map, map_far, places, rank):
    stacked = tile_map.shape[0] * rank
    shape = (stacked, len(places) * rank)
    tile, lane = lax.broadcasted_iota(jnp.int32, shape, 0), lax.broadcasted_iota(jnp.int32, shape, 1)
    same_row = tile % rank == lane % rank
    place = jnp.zeros(shape, jnp.int32)
    for i, o in enumerate(places):
        place = jnp.where(lane // rank == i, o, place)
    near, away = [
        jnp.broadcast_to((m ^ me)[:, :, None], (m.shape[0], rank, 1)).reshape(stacked, 1)
        for m in (tile_map, map_far)
    ]
    routes = [
        (same_row & (wanted == (place | side))).astype(bf16) for wanted in (near, away) for side in (0, core)
    ]
    square = (stacked, stacked)
    same = lax.broadcasted_iota(jnp.int32, square, 0) == lax.broadcasted_iota(jnp.int32, square, 1)
    return routes + [(same & ((near & far) != 0)).astype(bf16)]


def on_device(tokens, weight, bank_a, bank_b, tile_map, grad_out):
    blk_count = lax.axis_size("blk")
    tp_count = lax.axis_size("tp")
    me = lax.axis_index("blk")
    col = lax.axis_index("tp")
    offsets = list(range(0, blk_count, 4))
    bits = list(range(2, blk_count.bit_length() - 1))
    c_parts = 2

    rows = tokens.shape[0]
    features = tokens.shape[1]
    tile_count = tile_map.shape[0]
    tile_rows = rows // tile_count
    rank_two = bank_a.shape[2]
    rank_one = rank_two // 2
    kv_width = bank_b.shape[2]
    kv_dev = kv_width // tp_count
    local_rows = rows // tp_count
    stacked = tile_count * rank_two

    own_a = bank_a[0].T
    own_b = bank_b[0]
    map_far = swap(tile_map, far)
    keep = (
        lax.broadcasted_iota(jnp.int32, (stacked, rows), 0) // rank_two
        == lax.broadcasted_iota(jnp.int32, (stacked, rows), 1) // tile_rows
    )

    def split(value, count=rank_two):
        return [value[i : i + count] for i in range(0, value.shape[0], count)]

    places = [0]
    for bit in reversed(bits):
        places = places + [o | 1 << bit for o in places]

    def joined_hops(own):
        blocks, hops = own, []
        for bit in reversed(bits):
            more = swap(blocks, 1 << bit)
            hops.append(more)
            blocks = jnp.concatenate([blocks, more], axis=0)
        return blocks, hops

    def give_away(here, there):
        return (dot(far_here, here, (1, 0)) + dot(far_there, there, (1, 0))).astype(bf16)

    def take_in(here, there, got):
        return (
            dot(near_here, here, (1, 0)) + dot(near_there, there, (1, 0)) + dot(from_far, got, (1, 0))
        ).astype(bf16)

    def sums(sent, got, back):
        kept = dot(near_here, sent, (0, 0)) + dot(far_here, got, (0, 0)) + back.astype(f32)
        return dict(zip(places, split(kept)))

    def core_part(sent, got):
        return (dot(near_there, sent, (0, 0)) + dot(far_there, got, (0, 0))).astype(bf16)

    def leaving(total, bit):
        return jnp.concatenate([total[o].astype(bf16) for o in total if o >> bit & 1], axis=0)

    def add_hop(total, came, bit):
        gone = [o for o in total if o >> bit & 1]
        return {
            o ^ 1 << bit: total[o ^ 1 << bit] + c.astype(f32) for o, c in zip(gone, split(came))
        }

    if tp_count == 2:
        other = cross(grad_out)
        grad_rows = jnp.where(
            col == 0,
            jnp.concatenate([grad_out, other], axis=0),
            jnp.concatenate([other, grad_out], axis=0),
        )
    else:
        grad_rows = lax.all_gather(grad_out, "tp", axis=0, tiled=True)

    here_b, hops_b = joined_hops(own_b)
    near_here, near_there, far_here, far_there, from_far = plan(
        me, after(tile_map, hops_b[0]), after(map_far, hops_b[0]), places, rank_two
    )
    there_b = swap(here_b, core)
    sent_b = give_away(here_b, there_b)
    factor_b = take_in(here_b, there_b, swap(sent_b, far))
    key_row = lax.broadcasted_iota(jnp.int32, factor_b.shape, 0) % rank_two < rank_one
    nothing = jnp.zeros_like(factor_b)
    wide_b = jnp.concatenate(
        [jnp.where(key_row, factor_b, nothing), jnp.where(key_row, nothing, factor_b)], axis=1
    )
    rank_grad = jnp.where(keep, dot(wide_b, grad_rows, (1, 1)), 0.0).astype(bf16)
    width_c = features // c_parts
    down = [
        (adapter_scale * dot(rank_grad, tokens[:, i * width_c : (i + 1) * width_c], (1, 0))).astype(bf16)
        for i in range(c_parts)
    ]

    blocks_a = [after(own_a, sent_b)]
    late_hop = None
    for bit in reversed(bits):
        if len(blocks_a) > 1:
            blocks_a[-1] = late_hop = after(blocks_a[-1], down[0])
        blocks_a = blocks_a + [swap(block, 1 << bit) for block in blocks_a]
    here_a = jnp.concatenate(blocks_a, axis=0)
    half = features // 2
    base_low = dot(after(grad_rows, down[-1]), weight[:half], (1, 1))
    if tp_count == 2:
        base = dot(after(tokens, late_hop), weight, (1, 0))
        near_base = lax.dynamic_slice_in_dim(base, col * local_rows, local_rows, 0)
        far_base = lax.dynamic_slice_in_dim(base, (1 - col) * local_rows, local_rows, 0).astype(bf16)
    else:
        far_base = dot(tokens, weight, (1, 0))
        base_rows = lax.psum_scatter(far_base, "tp", scatter_dimension=0, tiled=True)
    here_a = after(here_a, far_base)
    there_a = swap(here_a, core)
    sent_a = give_away(here_a, there_a)

    if tp_count == 2:
        base_rows = near_base + cross(after(far_base, sent_a)).astype(f32)
    got_c = [after(swap(d, far), far_base) for d in down]
    back_c = [swap(core_part(d, g), core) for d, g in zip(down, got_c)]
    mark = sent_a
    total_c, came_c = [], []
    for sent, got, back in zip(down, got_c, back_c):
        total = sums(sent, got, after(back, sent_a))
        mark = after(leaving(total, bits[0]), mark)
        came_c.append(swap(mark, 1 << bits[0]))
        total_c.append(total)
    base_high = dot(after(grad_rows, mark), weight[half:], (1, 1))

    factor_a = take_in(here_a, there_a, after(swap(sent_a, far), base_high))
    rank_part = jnp.where(keep, dot(factor_a, tokens, (1, 1)), 0.0)
    rank_part = sum(split(rank_part))

    mark = rank_part
    ends = []
    for i, came in enumerate(came_c):
        total = add_hop(total_c[i], came, bits[0])
        for bit in bits[1:]:
            mark = after(leaving(total, bit), mark)
            came = swap(mark, 1 << bit)
            if bit == bits[-1]:
                ends.append((total, came))
            total = add_hop(total, came, bit)

    if tp_count == 2:
        rank_sum = rank_part + cross(rank_part)
    else:
        rank_sum = lax.psum(rank_part, "tp")
    rank_act = rank_sum.astype(bf16)

    first = col * local_rows
    local_act = lax.dynamic_slice_in_dim(rank_act, first, local_rows, 1)
    local_b = pick(split(wide_b), [first // tile_rows == k for k in range(tile_count)])
    key_value_output = (base_rows + adapter_scale * dot(local_act, local_b, (0, 0))).astype(bf16)

    spread = jnp.where(keep, jnp.concatenate([rank_act] * tile_count, axis=0), jnp.zeros((), bf16))
    whole = adapter_scale * dot(spread, grad_rows, (1, 0))
    key_part = lax.dynamic_slice(whole, (0, col * kv_dev), (stacked, kv_dev))
    value_part = lax.dynamic_slice(whole, (0, kv_width + col * kv_dev), (stacked, kv_dev))
    up = jnp.where(key_row[:, :kv_dev], key_part, value_part).astype(bf16)
    got_up = after(swap(up, far), mark)
    back_up = swap(core_part(up, got_up), core)
    total_up = sums(up, got_up, back_up)
    leave = [total_up[o].astype(bf16) for o in places[1:]]
    came_up = [swap(t, o) for o, t in zip(places[1:], leave)]
    grad_b = sum([c.astype(f32) for c in came_up], total_up[0])
    grad_a = jnp.concatenate(
        [add_hop(total, after(came, came_up[0]), bits[-1])[0] for total, came in ends], axis=1
    )

    late_grad = after(rank_grad, rank_act)
    token_gradient = jnp.concatenate(
        [
            (after(base, rank_act) + adapter_scale * dot(late_grad, factor, (0, 0))).astype(bf16)
            for base, factor in ((base_low, factor_a[:, :half]), (base_high, factor_a[:, half:]))
        ],
        axis=1,
    )
    return key_value_output, token_gradient, grad_a.T[None], grad_b[None]


def solution(mesh):
    in_specs = (
        P("blk", "tp"),
        P("tp", None),
        P("blk", "tp", None),
        P("blk", None, None),
        P("blk", None),
        P(("blk", "tp"), None),
    )
    out_specs = (P(("blk", "tp"), None), P("blk", "tp"), P("blk", "tp", None), P("blk", None, "tp"))
    return jax.shard_map(
        on_device, mesh=mesh, in_specs=in_specs, out_specs=out_specs, check_vma=False
    )
```

```python
import jax
import jax.numpy as jnp
from jax import lax
from jax.sharding import PartitionSpec as P

adapter_scale = 0.5
f32 = jnp.float32
bf16 = jnp.bfloat16
core, far = 1, 2


def swap(value, offset):
    count = lax.axis_size("blk")
    return lax.ppermute(value, "blk", [(i, i ^ offset) for i in range(count)])


def cross(value):
    return lax.ppermute(value, "tp", [(0, 1), (1, 0)])


def dot(a, b, contract):
    return lax.dot_general(a, b, ((contract[:1], contract[1:]), ((), ())), preferred_element_type=f32)


def pick(blocks, hits):
    out = jnp.where(hits[0], blocks[0], jnp.zeros_like(blocks[0]))
    for block, hit in zip(blocks[1:], hits[1:]):
        out = jnp.where(hit, block, out)
    return out


def blend(blocks, hits):
    out = jnp.zeros(blocks[0].shape, f32)
    for block, hit in zip(blocks, hits):
        out = out + jnp.where(hit, block.astype(f32), 0.0)
    return out


def after(value, *others):
    return lax.optimization_barrier((value,) + others)[0]


def plan(me, tile_map, map_far, places, rank):
    stacked = tile_map.shape[0] * rank
    shape = (stacked, len(places) * rank)
    tile, lane = lax.broadcasted_iota(jnp.int32, shape, 0), lax.broadcasted_iota(jnp.int32, shape, 1)
    same_row = tile % rank == lane % rank
    place = jnp.zeros(shape, jnp.int32)
    for i, o in enumerate(places):
        place = jnp.where(lane // rank == i, o, place)
    near, away = [
        jnp.broadcast_to((m ^ me)[:, :, None], (m.shape[0], rank, 1)).reshape(stacked, 1)
        for m in (tile_map, map_far)
    ]
    routes = [
        (same_row & (wanted == (place | side))).astype(bf16) for wanted in (near, away) for side in (0, core)
    ]
    square = (stacked, stacked)
    same = lax.broadcasted_iota(jnp.int32, square, 0) == lax.broadcasted_iota(jnp.int32, square, 1)
    return routes + [(same & ((near & far) != 0)).astype(bf16)]


def on_device(tokens, weight, bank_a, bank_b, tile_map, grad_out):
    blk_count = lax.axis_size("blk")
    tp_count = lax.axis_size("tp")
    me = lax.axis_index("blk")
    col = lax.axis_index("tp")
    offsets = list(range(0, blk_count, 4))
    bits = list(range(2, blk_count.bit_length() - 1))
    c_parts = 2

    rows = tokens.shape[0]
    features = tokens.shape[1]
    tile_count = tile_map.shape[0]
    tile_rows = rows // tile_count
    rank_two = bank_a.shape[2]
    rank_one = rank_two // 2
    kv_width = bank_b.shape[2]
    kv_dev = kv_width // tp_count
    local_rows = rows // tp_count
    stacked = tile_count * rank_two

    own_a = bank_a[0].T
    own_b = bank_b[0]
    map_far = swap(tile_map, far)
    keep = (
        lax.broadcasted_iota(jnp.int32, (stacked, rows), 0) // rank_two
        == lax.broadcasted_iota(jnp.int32, (stacked, rows), 1) // tile_rows
    )

    def split(value, count=rank_two):
        return [value[i : i + count] for i in range(0, value.shape[0], count)]

    places = [0]
    for bit in reversed(bits):
        places = places + [o | 1 << bit for o in places]

    def joined_hops(own):
        blocks, hops = own, []
        for bit in reversed(bits):
            more = swap(blocks, 1 << bit)
            hops.append(more)
            blocks = jnp.concatenate([blocks, more], axis=0)
        return blocks, hops

    def give_away(here, there):
        return (dot(far_here, here, (1, 0)) + dot(far_there, there, (1, 0))).astype(bf16)

    def take_in(here, there, got):
        return (
            dot(near_here, here, (1, 0)) + dot(near_there, there, (1, 0)) + dot(from_far, got, (1, 0))
        ).astype(bf16)

    def sums(sent, got, back):
        kept = near_part(sent)[half_rows:] + dot(far_here, got, (0, 0)) + back.astype(f32)
        return dict(zip(places, split(kept)))

    def core_part(sent, got):
        return (near_part(sent)[:half_rows] + dot(far_there, got, (0, 0))).astype(bf16)

    half_rows = len(places) * rank_two

    def near_part(sent):
        return dot(jnp.concatenate([near_there, near_here], axis=1), sent, (0, 0))

    def leaving(total, bit):
        return jnp.concatenate([total[o].astype(bf16) for o in total if o >> bit & 1], axis=0)

    def add_hop(total, came, bit):
        gone = [o for o in total if o >> bit & 1]
        return {
            o ^ 1 << bit: total[o ^ 1 << bit] + c.astype(f32) for o, c in zip(gone, split(came))
        }

    if tp_count == 2:
        other = cross(grad_out)
        grad_rows = jnp.where(
            col == 0,
            jnp.concatenate([grad_out, other], axis=0),
            jnp.concatenate([other, grad_out], axis=0),
        )
    else:
        grad_rows = lax.all_gather(grad_out, "tp", axis=0, tiled=True)

    here_b, hops_b = joined_hops(own_b)
    near_here, near_there, far_here, far_there, from_far = plan(
        me, after(tile_map, hops_b[0]), after(map_far, hops_b[0]), places, rank_two
    )
    there_b = swap(here_b, core)
    sent_b = give_away(here_b, there_b)
    factor_b = take_in(here_b, there_b, swap(sent_b, far))
    key_row = lax.broadcasted_iota(jnp.int32, factor_b.shape, 0) % rank_two < rank_one
    nothing = jnp.zeros_like(factor_b)
    wide_b = jnp.concatenate(
        [jnp.where(key_row, factor_b, nothing), jnp.where(key_row, nothing, factor_b)], axis=1
    )
    rank_grad = jnp.where(keep, dot(wide_b, grad_rows, (1, 1)), 0.0).astype(bf16)
    width_c = features // c_parts
    down = [
        (adapter_scale * dot(rank_grad, tokens[:, i * width_c : (i + 1) * width_c], (1, 0))).astype(bf16)
        for i in range(c_parts)
    ]

    blocks_a = [after(own_a, sent_b)]
    late_hop = None
    for bit in reversed(bits):
        if len(blocks_a) > 1:
            blocks_a[-1] = late_hop = after(blocks_a[-1], down[0])
        blocks_a = blocks_a + [swap(block, 1 << bit) for block in blocks_a]
    here_a = jnp.concatenate(blocks_a, axis=0)
    half = features // 2
    base_low = dot(after(grad_rows, down[-1]), weight[:half], (1, 1))
    if tp_count == 2:
        base = dot(after(tokens, late_hop), weight, (1, 0))
        near_base = lax.dynamic_slice_in_dim(base, col * local_rows, local_rows, 0)
        far_base = lax.dynamic_slice_in_dim(base, (1 - col) * local_rows, local_rows, 0).astype(bf16)
    else:
        far_base = dot(tokens, weight, (1, 0))
        base_rows = lax.psum_scatter(far_base, "tp", scatter_dimension=0, tiled=True)
    here_a = after(here_a, far_base)
    there_a = swap(here_a, core)
    sent_a = give_away(here_a, there_a)

    if tp_count == 2:
        base_rows = near_base + cross(after(far_base, sent_a)).astype(f32)
    got_c = [after(swap(d, far), far_base) for d in down]
    back_c = [swap(core_part(d, g), core) for d, g in zip(down, got_c)]
    mark = sent_a
    total_c, came_c = [], []
    for sent, got, back in zip(down, got_c, back_c):
        total = sums(sent, got, after(back, sent_a))
        mark = after(leaving(total, bits[0]), mark)
        came_c.append(swap(mark, 1 << bits[0]))
        total_c.append(total)
    base_high = dot(after(grad_rows, mark), weight[half:], (1, 1))

    factor_a = take_in(here_a, there_a, after(swap(sent_a, far), base_high))
    rank_part = jnp.where(keep, dot(factor_a, tokens, (1, 1)), 0.0)
    rank_part = sum(split(rank_part))

    mark = rank_part
    ends = []
    for i, came in enumerate(came_c):
        total = add_hop(total_c[i], came, bits[0])
        for bit in bits[1:]:
            mark = after(leaving(total, bit), mark)
            came = swap(mark, 1 << bit)
            if bit == bits[-1]:
                ends.append((total, came))
            total = add_hop(total, came, bit)

    if tp_count == 2:
        rank_sum = rank_part + cross(rank_part)
    else:
        rank_sum = lax.psum(rank_part, "tp")
    rank_act = rank_sum.astype(bf16)

    first = col * local_rows
    local_act = lax.dynamic_slice_in_dim(rank_act, first, local_rows, 1)
    local_b = pick(split(wide_b), [first // tile_rows == k for k in range(tile_count)])
    key_value_output = (base_rows + adapter_scale * dot(local_act, local_b, (0, 0))).astype(bf16)

    spread = jnp.where(keep, jnp.concatenate([rank_act] * tile_count, axis=0), jnp.zeros((), bf16))
    whole = adapter_scale * dot(spread, grad_rows, (1, 0))
    key_part = lax.dynamic_slice(whole, (0, col * kv_dev), (stacked, kv_dev))
    value_part = lax.dynamic_slice(whole, (0, kv_width + col * kv_dev), (stacked, kv_dev))
    up = jnp.where(key_row[:, :kv_dev], key_part, value_part).astype(bf16)
    got_up = after(swap(up, far), mark)
    back_up = swap(core_part(up, got_up), core)
    total_up = sums(up, got_up, back_up)
    leave = [total_up[o].astype(bf16) for o in places[1:]]
    came_up = [swap(t, o) for o, t in zip(places[1:], leave)]
    grad_b = sum([c.astype(f32) for c in came_up], total_up[0])
    grad_a = jnp.concatenate(
        [add_hop(total, after(came, came_up[0]), bits[-1])[0] for total, came in ends], axis=1
    )

    late_grad = after(rank_grad, rank_act)
    token_gradient = jnp.concatenate(
        [
            (after(base, rank_act) + adapter_scale * dot(late_grad, factor, (0, 0))).astype(bf16)
            for base, factor in ((base_low, factor_a[:, :half]), (base_high, factor_a[:, half:]))
        ],
        axis=1,
    )
    return key_value_output, token_gradient, grad_a.T[None], grad_b[None]


def solution(mesh):
    in_specs = (
        P("blk", "tp"),
        P("tp", None),
        P("blk", "tp", None),
        P("blk", None, None),
        P("blk", None),
        P(("blk", "tp"), None),
    )
    out_specs = (P(("blk", "tp"), None), P("blk", "tp"), P("blk", "tp", None), P("blk", None, "tp"))
    return jax.shard_map(
        on_device, mesh=mesh, in_specs=in_specs, out_specs=out_specs, check_vma=False
    )
```
